256 devices in a mesh: ctx: 64 (over x_hi, y, z), head: 4 (over x_lo, core).
Axes of the slice: x: 4 (x_hi: 2, x_lo: 2; x = x_hi * 2 + x_lo), y: 4, z: 8, core: 2. Of those that a mesh axis runs over, the one named last changes fastest.
Arguments:
- queries: bfloat16 [8192, 4096], P('ctx', 'head'), may hold values from -9 to 9
- keys: bfloat16 [8192, 512], P('ctx', 'head'), may hold values from -9 to 9
- values: bfloat16 [8192, 512], P('ctx', 'head'), may hold values from -6 to 6
- doc_lengths: int32 [8], replicated, may hold values from 1 to 2048, 8192 in all
- source_row: int32 [64, 128], replicated, may hold values from 0 to 8191, as said below
Outputs:
- attn_out: bfloat16 [8192, 4096], P('ctx', 'head')
- max_logits: float32 [32, 8], replicated
The draws below stay inside these ranges and needn't reach their ends.
Inputs may be any that keep to these rules, and one draw needn't show every extreme that they name: source_row[d, c * 2 + s] lies in c * 128 .. (c + 1) * 128 - 1 for every d, every c in 0 .. 63 and s in 0 .. 1; every row 0 .. 8191 appears exactly once.
All inputs are finite; a program needn't handle non-finite values.
Results may differ from the reference program's by a relative error of at most 0.007.
Values may be sent and summed in bfloat16 or wider, within the bound.
No kernel may reach another device: no remote copies, remote signals or barrier semaphores. Data moves between devices by JAX's collectives and lax.ppermute only.
A program may use at most 64 MiB of HBM per device.

```python
import math
import jax
import jax.numpy as jnp
import numpy as np
from jax import lax

HD = 128
QH = 32
KVH = 4
DOCS = 8
TOK_DEV = 128
TOKENS = 8192


def shared_keys(key):
    base = jnp.clip(jax.random.normal(jax.random.fold_in(key, 11), (TOKENS, KVH * HD), jnp.float32), -4.0, 4.0)
    return (base, jnp.zeros((TOKENS,), dtype=bool))


def draw_keys(key, part):
    return shared_keys(key)[0].astype(jnp.bfloat16)


def draw_queries(key, part):
    keys_full, special = shared_keys(key)
    base = jnp.clip(jax.random.normal(jax.random.fold_in(key, 12), (TOKENS, QH * HD), jnp.float32), -4.0, 4.0)
    group_size = QH // KVH
    copied = jnp.broadcast_to(keys_full.reshape(TOKENS, KVH, 1, HD), (TOKENS, KVH, group_size, HD)).reshape(TOKENS, QH * HD)
    return jnp.where(special[:, None], copied, base).astype(jnp.bfloat16)


def draw_source_row(key, part):
    senders = TOKENS // TOK_DEV
    per_peer = TOK_DEV // senders
    sub_keys = jax.random.split(jax.random.fold_in(key, 21), senders)
    ordering = jax.vmap(lambda sub_key: jax.random.permutation(sub_key, TOK_DEV))(sub_keys)
    arranged = ordering.reshape(senders, senders, per_peer) + (jnp.arange(senders) * TOK_DEV)[:, None, None]
    return jnp.transpose(arranged, (1, 0, 2)).reshape(senders, TOK_DEV).astype(jnp.int32)


def levels(stream_key, shape, pieces, least, top_value):
    def one(axis_at, shards_of):
        draws = jax.random.uniform(jax.random.fold_in(jax.random.fold_in(stream_key, 6), axis_at), (shards_of,), jnp.float32, least / len(pieces), top_value / len(pieces))
        return jnp.repeat(jnp.exp(draws), shape[axis_at] // shards_of).reshape((-1,) + (1,) * (len(shape) - axis_at - 1))

    loudness = one(*pieces[0])
    for cut in pieces[1:]:
        loudness = loudness * one(*cut)
    return loudness


def profile(number_of, total, limit, slope):
    weights = [(1 << 20) // math.isqrt(standing ** slope) + 1 for standing in range(2, number_of + 1)]
    spare, counts = total - limit - (number_of - 1), [1] * (number_of - 1)
    while spare > 0:
        candidates = [i for i in range(number_of - 1) if counts[i] < limit]
        whole, left = sum([weights[i] for i in candidates]), spare
        for i in candidates:
            extra = min(limit - counts[i], max(1, left * weights[i] // whole), spare)
            counts[i] = counts[i] + extra
            spare = spare - extra
    return np.array([limit] + counts)


def ragged_sizes(own_key, amount, total, bound, skew):
    if amount == 2:
        one = jax.random.randint(own_key, (), max(1, total - bound), min(bound, total - 1) + 1)
        return jnp.stack([one, total - one])
    sizes = jnp.asarray(profile(amount, total, bound, skew), jnp.int32)
    twos = (amount - 1) // 2
    source_of, sink = sizes[1:1 + 2 * twos:2], sizes[2:2 + 2 * twos:2]
    slack = jnp.minimum(source_of - 1, bound - sink)
    moved = jax.random.randint(jax.random.fold_in(own_key, 1), (twos,), 0, 1 << 20) % (slack + 1)
    sizes = sizes.at[1:1 + 2 * twos:2].set(source_of - moved).at[2:2 + 2 * twos:2].set(sink + moved)
    return sizes[jax.random.permutation(jax.random.fold_in(own_key, 2), amount)]


def normal_values(stream_key, shape, deviation, limit, shards=(), kind=jnp.bfloat16):
    level = levels(stream_key, shape, shards, -0.22, 0.18) if shards else 1.0
    entries = jax.random.normal(stream_key, shape, jnp.float32) * deviation * level
    return jnp.minimum(jnp.maximum(entries, -limit), limit).astype(kind)


def setup_inputs(seed: int = 0) -> dict:
    splits = jax.random.split(jax.random.key(seed), 6)
    return {
        "queries": draw_queries(jax.random.fold_in(splits[5], 71), 0),
        "keys": draw_keys(jax.random.fold_in(splits[5], 71), 0),
        "values": normal_values(splits[2], (TOKENS, KVH * HD), 1.0, 6.0, ((0, 64), (1, 4))),
        "doc_lengths": ragged_sizes(splits[3], DOCS, TOKENS, TOKENS // 4, 2).astype(jnp.int32),
        "source_row": draw_source_row(jax.random.fold_in(splits[5], 71), 0),
    }


NEG_BIG = -1e+30

def reference(queries, keys, values, doc_lengths, source_row):
    group_size = QH // KVH
    positions = jnp.arange(TOKENS, dtype=jnp.int32)
    doc_ends = jnp.cumsum(doc_lengths).astype(jnp.int32)
    row_docs = lax.optimization_barrier(jnp.sum((positions[:, None] >= doc_ends[None, :]).astype(jnp.int32), axis=1)).astype(jnp.int32)
    key_heads = keys.astype(jnp.float32).reshape(TOKENS, KVH, HD)
    value_heads = values.astype(jnp.float32).reshape(TOKENS, KVH, HD)
    query_heads = queries.reshape(TOKENS, KVH, group_size, HD)
    block_len = min(128, TOKENS)
    inv_root = 1.0 / math.sqrt(HD)

    def one_block(block_no):
        first_row = (block_no * block_len).astype(jnp.int32)
        query_block = lax.dynamic_slice_in_dim(query_heads, first_row, block_len, 0).astype(jnp.float32)
        block_pos = lax.dynamic_slice_in_dim(positions, first_row, block_len, 0)
        block_docs = lax.dynamic_slice_in_dim(row_docs, first_row, block_len, 0)
        allowed = (block_docs[:, None] == row_docs[None, :]) & (positions[None, :] <= block_pos[:, None])
        live_mask = allowed[:, None, None, :]
        scores = jnp.einsum('tkgd,jkd->tkgj', query_block, key_heads, precision=lax.Precision.HIGHEST) * inv_root
        scores = jnp.where(live_mask, scores, NEG_BIG)
        row_max = lax.optimization_barrier(jnp.max(scores, axis=3))
        exponent = jnp.where(live_mask, jnp.exp(scores - row_max[..., None]), 0.0)
        row_total = lax.optimization_barrier(jnp.sum(exponent, axis=3))
        rounded = lax.optimization_barrier(exponent.astype(jnp.bfloat16)).astype(jnp.float32)
        context = jnp.einsum('tkgj,jkd->tkgd', rounded, value_heads, precision=lax.Precision.HIGHEST) / row_total[..., None]
        context = context.astype(jnp.bfloat16).reshape(block_len, QH * HD)
        doc_hit = block_docs[:, None] == jnp.arange(DOCS, dtype=jnp.int32)[None, :]
        block_max = lax.optimization_barrier(jnp.max(jnp.where(doc_hit[:, None, :], row_max.reshape(block_len, QH)[:, :, None], NEG_BIG), axis=0))
        return (context, block_max)
    contexts, maxima = lax.map(one_block, jnp.arange(TOKENS // block_len, dtype=jnp.int32))
    context_all = contexts.reshape(TOKENS, QH * HD)
    attn_out = jnp.take(context_all, source_row.reshape(-1).astype(jnp.int32), axis=0)
    return (attn_out, lax.optimization_barrier(jnp.max(maxima, axis=0)))
```

```python
import functools
import math

import jax
import jax.numpy as jnp
from jax import lax
from jax.experimental import pallas as pl
from jax.experimental.pallas import tpu as pltpu
from jax.sharding import PartitionSpec as P

HD = 128
HEADS = 8
DOCS = 8
ROWS = 128
GROUP = 16
CTX = 64
NEG_BIG = -1e30
SCALE = 1.0 / math.sqrt(HD)
SCALE_LOG2E = SCALE * math.log2(math.e)
HEADS_AT_ONCE = 2


def dot_nt(a, b):
    return lax.dot_general(a, b, (((1,), (1,)), ((), ())), preferred_element_type=jnp.float32)


def attend_kernel(lengths_ref, source_ref, q_ref, kv_ref, own_ref, out_ref, bias_ref, q_scr):
    me = lax.axis_index("ctx")
    lane = lax.broadcasted_iota(jnp.int32, (ROWS, 128), 1)
    row = lax.broadcasted_iota(jnp.int32, (ROWS, 128), 0)
    chunk_lane = lax.broadcasted_iota(jnp.int32, (CTX, 128), 1) // 2
    local = (source_ref[...] - chunk_lane * ROWS).astype(jnp.float32).astype(jnp.bfloat16)
    spread = (
        lax.broadcasted_iota(jnp.int32, (ROWS, CTX), 0) // 2
        == lax.broadcasted_iota(jnp.int32, (ROWS, CTX), 1)
    ).astype(jnp.float32).astype(jnp.bfloat16)
    table = jnp.dot(spread, local, preferred_element_type=jnp.float32)
    wanted = lane == 2 * me + row % 2
    pick = jnp.sum(jnp.where(wanted, table, 0.0), axis=1, keepdims=True).astype(jnp.int32)
    one_hot = (lane == pick).astype(jnp.float32).astype(jnp.bfloat16)
    q_all = jnp.dot(one_hot, q_ref[...], preferred_element_type=jnp.float32)
    for h in range(HEADS):
        q_scr[h * ROWS : (h + 1) * ROWS, :] = q_all[:, h * HD : (h + 1) * HD].astype(jnp.bfloat16)

    pos = me * ROWS + pick
    start = jnp.zeros_like(pos)
    doc = jnp.zeros_like(pos)
    end = jnp.int32(0)
    for i in range(DOCS):
        end = end + lengths_ref[i]
        passed = pos >= end
        start = jnp.where(passed, end, start)
        doc = doc + passed.astype(jnp.int32)
    in_group = me % GROUP
    base = me - in_group
    for j in range(GROUP + 1):
        if j < GROUP:
            block = base + j - jnp.where(j >= in_group, GROUP, 0)
        else:
            block = me
        key_pos = block * ROWS + lane
        ok = (key_pos >= start) & (key_pos <= pos)
        bias_ref[:, j * 128 : (j + 1) * 128] = jnp.where(ok, 0.0, NEG_BIG)

    keys = kv_ref[:, :HD]
    values = kv_ref[:, HD:]
    own_keys = own_ref[:, :HD]
    own_values = own_ref[:, HD:]
    far = GROUP * ROWS
    best = jnp.full((ROWS, 128), NEG_BIG, jnp.float32)
    n = HEADS_AT_ONCE
    for h0 in range(0, HEADS, n):
        q = q_scr[h0 * ROWS : (h0 + n) * ROWS, :]
        s_far = dot_nt(q, keys).reshape(n, ROWS, far) + bias_ref[:, :far][None]
        s_own = dot_nt(q, own_keys).reshape(n, ROWS, ROWS) + bias_ref[:, far:][None]
        top = jnp.maximum(
            jnp.max(s_far, axis=2, keepdims=True), jnp.max(s_own, axis=2, keepdims=True)
        )
        w_far = jnp.exp2((s_far - top) * SCALE_LOG2E)
        w_own = jnp.exp2((s_own - top) * SCALE_LOG2E)
        total = jnp.sum(w_far, axis=2, keepdims=True) + jnp.sum(w_own, axis=2, keepdims=True)
        acc = jnp.dot(
            w_far.astype(jnp.bfloat16).reshape(n * ROWS, far),
            values,
            preferred_element_type=jnp.float32,
        ) + jnp.dot(
            w_own.astype(jnp.bfloat16).reshape(n * ROWS, ROWS),
            own_values,
            preferred_element_type=jnp.float32,
        )
        context = acc.reshape(n, ROWS, HD) / total
        for k in range(n):
            h = h0 + k
            out_ref[:, h * HD : (h + 1) * HD] = context[k].astype(jnp.bfloat16)
            hit = lane % 64 == h * DOCS + doc
            best = jnp.maximum(best, jnp.where(hit, top[k] * SCALE, NEG_BIG))
    most = jnp.max(best, axis=0, keepdims=True)
    first = most.astype(jnp.bfloat16).astype(jnp.float32)
    second = (most - first).astype(jnp.bfloat16).astype(jnp.float32)
    third = most - first - second
    low = lane < 64
    even = row % 2 == 0
    parts = jnp.where(even, jnp.where(low, first, second), jnp.where(low, third, 0.0))
    out_ref[:, HEADS * HD :] = parts.astype(jnp.bfloat16)


def attend(doc_lengths, source_row, queries, kv_window, kv_own):
    vmem = pl.BlockSpec(memory_space=pltpu.VMEM)
    return pl.pallas_call(
        attend_kernel,
        out_shape=jax.ShapeDtypeStruct((ROWS, HEADS * HD + 128), jnp.bfloat16),
        in_specs=[pl.BlockSpec(memory_space=pltpu.SMEM), vmem, vmem, vmem, vmem],
        out_specs=vmem,
        scratch_shapes=[
            pltpu.VMEM((ROWS, (GROUP + 1) * ROWS), jnp.float32),
            pltpu.VMEM((HEADS * ROWS, HD), jnp.bfloat16),
        ],
        compiler_params=pltpu.CompilerParams(vmem_limit_bytes=40 * 1024 * 1024),
        name="attend",
    )(doc_lengths, source_row, queries, kv_window, kv_own)


def body(queries, keys, values, doc_lengths, source_row):
    me = lax.axis_index("ctx")
    own = jnp.concatenate([keys, values], axis=1)
    before = lax.ppermute(own, "ctx", [(c, c + GROUP) for c in range(CTX - GROUP)])
    groups = [[g * GROUP + i for i in range(GROUP)] for g in range(CTX // GROUP)]
    later = jnp.arange(GROUP, dtype=jnp.int32) > me % GROUP
    slots = jnp.where(later[:, None, None], own[None], before[None])
    window = lax.all_to_all(
        slots, "ctx", split_axis=0, concat_axis=0, tiled=True, axis_index_groups=groups
    ).reshape(GROUP * ROWS, 2 * HD)
    sent = attend(doc_lengths, source_row, queries, window, own)
    got = lax.all_to_all(
        sent.reshape(CTX, 2, HEADS * HD + 128), "ctx", split_axis=0, concat_axis=0, tiled=True
    )
    context = got[:, :, : HEADS * HD].reshape(ROWS, HEADS * HD)
    parts = got[:, :, HEADS * HD :].astype(jnp.float32)
    maxima = jnp.max(parts[:, 0, :64] + (parts[:, 0, 64:] + parts[:, 1, :64]), axis=0)
    all_maxima = lax.all_gather(maxima.reshape(HEADS, DOCS), "head", axis=0, tiled=True)
    return (context, all_maxima)


def solution(mesh):
    return jax.shard_map(
        body,
        mesh=mesh,
        in_specs=(P("ctx", "head"), P("ctx", "head"), P("ctx", "head"), P(), P()),
        out_specs=(P("ctx", "head"), P()),
        check_vma=False,
    )
```

```python
import math

import jax
import jax.numpy as jnp
from jax import lax
from jax.experimental import pallas as pl
from jax.experimental.pallas import tpu as pltpu
from jax.sharding import PartitionSpec as P

HD = 128
HEADS = 8
DOCS = 8
ROWS = 128
RING = 8
CTX = 64
WIDE = HEADS * HD
PART = WIDE + 128
NEG_BIG = -1e30
SCALE = 1.0 / math.sqrt(HD)
SCALE_LOG2E = SCALE * math.log2(math.e)
HEADS_AT_ONCE = 2
FAR = RING * ROWS


def dot_nt(a, b):
    return lax.dot_general(a, b, (((1,), (1,)), ((), ())), preferred_element_type=jnp.float32)


def as_bf16(mask):
    return mask.astype(jnp.float32).astype(jnp.bfloat16)


def three_parts(x):
    first = x.astype(jnp.bfloat16).astype(jnp.float32)
    second = (x - first).astype(jnp.bfloat16).astype(jnp.float32)
    return first, second, x - first - second


def iota(shape, dim):
    return lax.broadcasted_iota(jnp.int32, shape, dim)


def attend_kernel(
    lengths_ref, source_ref, q_ref, next_q_ref, kv_ref, own_ref, out_ref, bias_ref, q_scr
):
    me = lax.axis_index("ctx")
    lane = iota((ROWS, 128), 1)
    row = iota((ROWS, 128), 0)
    local = as_bf16(source_ref[...] - iota((CTX, 128), 1) // 2 * ROWS)
    spread = as_bf16(iota((ROWS, CTX), 0) // 2 == iota((ROWS, CTX), 1))
    table = jnp.dot(spread, local, preferred_element_type=jnp.float32)
    in_ring = me % RING
    base = me - in_ring
    best = jnp.full((ROWS, 128), NEG_BIG, jnp.float32)
    logs = []
    n = HEADS_AT_ONCE
    for part, rows_ref in ((0, q_ref), (1, next_q_ref)):
        chunk = me + RING * part
        pick = jnp.sum(
            jnp.where(lane == 2 * chunk + row % 2, table, 0.0), axis=1, keepdims=True
        ).astype(jnp.int32)
        q_all = jnp.dot(as_bf16(lane == pick), rows_ref[...], preferred_element_type=jnp.float32)
        for h in range(HEADS):
            q_scr[h * ROWS : (h + 1) * ROWS, :] = q_all[:, h * HD : (h + 1) * HD].astype(
                jnp.bfloat16
            )
        pos = chunk * ROWS + pick
        start = jnp.zeros_like(pos)
        doc = jnp.zeros_like(pos)
        end = jnp.int32(0)
        for i in range(DOCS):
            end = end + lengths_ref[i]
            passed = pos >= end
            start = jnp.where(passed, end, start)
            doc = doc + passed.astype(jnp.int32)
        for j in range(RING + 1):
            if j < RING:
                block = base + j - jnp.where(j >= in_ring, RING, 0)
            else:
                block = me
            key_pos = block * ROWS + lane
            ok = (key_pos >= start) & (key_pos <= pos)
            if part == 0:
                ok = ok & (block > me - RING)
            bias_ref[:, j * 128 : (j + 1) * 128] = jnp.where(ok, 0.0, NEG_BIG)

        log_total = jnp.zeros((ROWS, 128), jnp.float32)
        for h0 in range(0, HEADS, n):
            q = q_scr[h0 * ROWS : (h0 + n) * ROWS, :]
            s_far = dot_nt(q, kv_ref[:, :HD]).reshape(n, ROWS, FAR) + bias_ref[:, :FAR][None]
            s_own = dot_nt(q, own_ref[:, :HD]).reshape(n, ROWS, ROWS) + bias_ref[:, FAR:][None]
            top = jnp.maximum(
                jnp.max(s_far, axis=2, keepdims=True), jnp.max(s_own, axis=2, keepdims=True)
            )
            w_far = jnp.exp2((s_far - top) * SCALE_LOG2E)
            w_own = jnp.exp2((s_own - top) * SCALE_LOG2E)
            total = jnp.sum(w_far, axis=2, keepdims=True) + jnp.sum(w_own, axis=2, keepdims=True)
            acc = jnp.dot(
                w_far.astype(jnp.bfloat16).reshape(n * ROWS, FAR),
                kv_ref[:, HD:],
                preferred_element_type=jnp.float32,
            ) + jnp.dot(
                w_own.astype(jnp.bfloat16).reshape(n * ROWS, ROWS),
                own_ref[:, HD:],
                preferred_element_type=jnp.float32,
            )
            context = acc.reshape(n, ROWS, HD) / total
            for k in range(n):
                h = h0 + k
                at = part * PART + h * HD
                out_ref[:, at : at + HD] = context[k].astype(jnp.bfloat16)
                peak = top[k] * SCALE
                best = jnp.maximum(
                    best, jnp.where(lane == h * DOCS + doc, peak, NEG_BIG)
                )
                log_total = jnp.where(lane % 8 == h, peak + jnp.log(total[k]), log_total)
        logs.append(log_total)

    most = three_parts(jnp.max(best, axis=0, keepdims=True))
    even = row % 2 == 0
    for part in range(2):
        first, second, third = three_parts(logs[part])
        tail = jnp.where(lane < 72, first, jnp.where(lane < 80, second, third))
        if part == 0:
            head = jnp.where(even, most[0], most[1])
        else:
            head = jnp.where(even, most[2], 0.0)
        at = part * PART + WIDE
        out_ref[:, at : at + 128] = jnp.where(lane < 64, head, tail).astype(jnp.bfloat16)


def merge_kernel(got_ref, out_ref, maxima_ref):
    lane = iota((ROWS, 128), 1)
    row = iota((ROWS, 128), 0)
    shift = 2 * RING
    near = got_ref[:, WIDE : WIDE + 128].astype(jnp.float32)
    far = got_ref[:, PART + WIDE : PART + WIDE + 128].astype(jnp.float32)

    most = near + (pltpu.roll(near, ROWS - 1, 0) + far)
    most = jnp.max(jnp.where(row % 2 == 0, most, NEG_BIG), axis=0, keepdims=True)
    lane8 = iota((HEADS, 128), 1)
    spread = jnp.where(lane8 // DOCS == iota((HEADS, 128), 0), most, 0.0)
    fold = as_bf16(
        (iota((128, DOCS), 0) % DOCS == iota((128, DOCS), 1)) & (iota((128, DOCS), 0) < 64)
    )
    folded = [
        jnp.dot(p.astype(jnp.bfloat16), fold, preferred_element_type=jnp.float32)
        for p in three_parts(spread)
    ]
    maxima_ref[...] = folded[0] + (folded[1] + folded[2])

    def whole(x):
        return x + (pltpu.roll(x, 128 - 8, 1) + pltpu.roll(x, 128 - 16, 1))

    log_near = whole(near)
    log_far = pltpu.roll(whole(far), shift, 0)
    weight = 1.0 / (1.0 + jnp.exp(log_far - log_near))
    weight = jnp.where(row < shift, 1.0, weight)
    for h in range(HEADS):
        w = weight[:, 64 + h : 65 + h]
        mine = got_ref[:, h * HD : (h + 1) * HD].astype(jnp.float32)
        other = got_ref[:, PART + h * HD : PART + (h + 1) * HD].astype(jnp.float32)
        other = pltpu.roll(other, shift, 0)
        out_ref[:, h * HD : (h + 1) * HD] = (mine * w + other * (1.0 - w)).astype(jnp.bfloat16)


VMEM = pl.BlockSpec(memory_space=pltpu.VMEM)
SMEM = pl.BlockSpec(memory_space=pltpu.SMEM)


def attend(doc_lengths, source_row, queries, next_queries, window, own):
    return pl.pallas_call(
        attend_kernel,
        out_shape=jax.ShapeDtypeStruct((ROWS, 2 * PART), jnp.bfloat16),
        in_specs=[SMEM, VMEM, VMEM, VMEM, VMEM, VMEM],
        out_specs=VMEM,
        scratch_shapes=[
            pltpu.VMEM((ROWS, FAR + ROWS), jnp.float32),
            pltpu.VMEM((HEADS * ROWS, HD), jnp.bfloat16),
        ],
        compiler_params=pltpu.CompilerParams(vmem_limit_bytes=40 * 1024 * 1024),
        name="attend",
    )(doc_lengths, source_row, queries, next_queries, window, own)


def merge(got):
    return pl.pallas_call(
        merge_kernel,
        out_shape=(
            jax.ShapeDtypeStruct((ROWS, WIDE), jnp.bfloat16),
            jax.ShapeDtypeStruct((HEADS, DOCS), jnp.float32),
        ),
        in_specs=[VMEM],
        out_specs=(VMEM, VMEM),
        compiler_params=pltpu.CompilerParams(vmem_limit_bytes=40 * 1024 * 1024),
        name="merge",
    )(got)


def body(queries, keys, values, doc_lengths, source_row):
    me = lax.axis_index("ctx")
    own = jnp.concatenate([keys, values], axis=1)
    before = lax.ppermute(own, "ctx", [(c, c + RING) for c in range(CTX - RING)])
    next_queries = lax.ppermute(queries, "ctx", [(c + RING, c) for c in range(CTX - RING)])
    rings = [[r * RING + i for i in range(RING)] for r in range(CTX // RING)]
    later = jnp.arange(RING, dtype=jnp.int32) > me % RING
    slots = jnp.where(later[:, None, None], own[None], before[None])
    window = lax.all_to_all(
        slots, "ctx", split_axis=0, concat_axis=0, tiled=True, axis_index_groups=rings
    ).reshape(FAR, 2 * HD)
    sent = attend(doc_lengths, source_row, queries, next_queries, window, own)
    got = lax.all_to_all(
        sent.reshape(CTX, 2, 2 * PART), "ctx", split_axis=0, concat_axis=0, tiled=True
    )
    context, maxima = merge(got.reshape(ROWS, 2 * PART))
    all_maxima = lax.all_gather(maxima, "head", axis=0, tiled=True)
    return (context, all_maxima)


def solution(mesh):
    return jax.shard_map(
        body,
        mesh=mesh,
        in_specs=(P("ctx", "head"), P("ctx", "head"), P("ctx", "head"), P(), P()),
        out_specs=(P("ctx", "head"), P()),
        check_vma=False,
    )
```

```python
import math

import jax
import jax.numpy as jnp
from jax import lax
from jax.experimental import pallas as pl
from jax.experimental.pallas import tpu as pltpu
from jax.sharding import PartitionSpec as P

HD = 128
HEADS = 8
GROUPS = 4
DOCS = 8
ROWS = 128
RING = 8
RINGS = 8
CTX = RING * RINGS
PARTS = 2
WIDE = HEADS * HD
FAR = RING * ROWS
WINDOW = FAR + ROWS
NEG_BIG = -1e30
SCALE = 1.0 / math.sqrt(HD)
SCALE_LOG2E = SCALE * math.log2(math.e)
HEADS_AT_ONCE = 4
SPAN = GROUPS * HEADS


def dot_nt(a, b):
    return lax.dot_general(a, b, (((1,), (1,)), ((), ())), preferred_element_type=jnp.float32)


def as_bf16(mask):
    return mask.astype(jnp.float32).astype(jnp.bfloat16)


def three_parts(x):
    first = x.astype(jnp.bfloat16).astype(jnp.float32)
    second = (x - first).astype(jnp.bfloat16).astype(jnp.float32)
    return first, second, x - first - second


def iota(shape, dim):
    return lax.broadcasted_iota(jnp.int32, shape, dim)


def prepare_kernel(
    lengths_ref, source_ref, q0_ref, q1_ref, q_out, bias_out, doc_out
):
    me = lax.axis_index("ctx")
    lane = iota((ROWS, 128), 1)
    row = iota((ROWS, 128), 0)
    local = as_bf16(source_ref[...] - iota((CTX, 128), 1) // 2 * ROWS)
    spread = as_bf16(iota((ROWS, CTX), 0) // 2 == iota((ROWS, CTX), 1))
    table = jnp.dot(spread, local, preferred_element_type=jnp.float32)
    in_ring = me % RING
    base = me - in_ring
    for part, rows_ref in enumerate((q0_ref, q1_ref)):
        chunk = me + RING * part
        pick = jnp.sum(
            jnp.where(lane == 2 * chunk + row % 2, table, 0.0), axis=1, keepdims=True
        ).astype(jnp.int32)
        q_all = jnp.dot(as_bf16(lane == pick), rows_ref[...], preferred_element_type=jnp.float32)
        for h in range(HEADS):
            q_out[part, h * ROWS : (h + 1) * ROWS, :] = q_all[:, h * HD : (h + 1) * HD].astype(
                jnp.bfloat16
            )
        pos = chunk * ROWS + pick
        start = jnp.zeros_like(pos)
        doc = jnp.zeros_like(pos)
        end = jnp.int32(0)
        for i in range(DOCS):
            end = end + lengths_ref[i]
            passed = pos >= end
            start = jnp.where(passed, end, start)
            doc = doc + passed.astype(jnp.int32)
        doc_out[part] = jnp.broadcast_to(doc, (ROWS, 128))
        for j in range(RING + 1):
            block = me if j == RING else base + j - jnp.where(j >= in_ring, RING, 0)
            key_pos = block * ROWS + lane
            ok = (key_pos >= start) & (key_pos <= pos)
            if part == 0:
                ok = ok & (block > me - RING)
            bias_out[part, :, j * 128 : (j + 1) * 128] = jnp.where(ok, 0.0, NEG_BIG)


def attend_kernel(q_ref, bias_ref, doc_ref, kv_ref, own_ref, out_ref):
    lane = iota((ROWS, 128), 1)
    n = HEADS_AT_ONCE
    all_logs = []
    best = jnp.full((ROWS, 128), NEG_BIG, jnp.float32)
    for part in range(PARTS):
        peaks = jnp.full((ROWS, 128), NEG_BIG, jnp.float32)
        logs = jnp.full((ROWS, 128), NEG_BIG, jnp.float32)
        for h0 in range(0, HEADS, n):
            q = q_ref[part, h0 * ROWS : (h0 + n) * ROWS, :]
            s_far = dot_nt(q, kv_ref[:, :HD]).reshape(n, ROWS, FAR) + bias_ref[part, :, :FAR][None]
            s_own = (
                dot_nt(q, own_ref[:, :HD]).reshape(n, ROWS, ROWS) + bias_ref[part, :, FAR:][None]
            )
            top = jnp.maximum(
                jnp.max(s_far, axis=2, keepdims=True), jnp.max(s_own, axis=2, keepdims=True)
            )
            w_far = jnp.exp2((s_far - top) * SCALE_LOG2E)
            w_own = jnp.exp2((s_own - top) * SCALE_LOG2E)
            total = jnp.sum(w_far, axis=2, keepdims=True) + jnp.sum(w_own, axis=2, keepdims=True)
            acc = jnp.dot(
                w_far.astype(jnp.bfloat16).reshape(n * ROWS, FAR),
                kv_ref[:, HD:],
                preferred_element_type=jnp.float32,
            ) + jnp.dot(
                w_own.astype(jnp.bfloat16).reshape(n * ROWS, ROWS),
                own_ref[:, HD:],
                preferred_element_type=jnp.float32,
            )
            context = acc.reshape(n, ROWS, HD) / total
            for k in range(n):
                h = h0 + k
                at = part * WIDE + h * HD
                out_ref[:, at : at + HD] = context[k].astype(jnp.bfloat16)
                peak = top[k] * SCALE
                peaks = jnp.where(lane % 8 == h, peak, peaks)
                logs = jnp.where(lane % 8 == h, peak + jnp.log(total[k]), logs)
        all_logs.append(logs)
        best = jnp.maximum(best, jnp.where(lane // 8 == doc_ref[part], peaks, NEG_BIG))

    logs = jnp.where(lane < 24, all_logs[0], all_logs[1])
    step = lane % 24 // 8
    pieces = three_parts(logs)
    tail = jnp.where(step == 0, pieces[0], jnp.where(step == 1, pieces[1], pieces[2]))
    most = three_parts(pltpu.roll(jnp.max(best, axis=0, keepdims=True), 48, 1))
    maxima = jnp.where(iota((ROWS, 128), 0) % 2 == 0, most[0], most[1])
    tail = jnp.where(lane < 48, tail, jnp.where(lane < 112, maxima, 0.0))
    out_ref[:, PARTS * WIDE :] = tail.astype(jnp.bfloat16)


def merge_kernel(got_ref, out_ref, maxima_ref):
    row = iota((ROWS, 128), 0)
    tail = got_ref[:, PARTS * WIDE :].astype(jnp.float32)

    most = tail + pltpu.roll(tail, ROWS - 1, 0)
    most = jnp.max(jnp.where(row % 2 == 0, most, NEG_BIG), axis=0, keepdims=True)
    lane_d = iota((DOCS, 128), 1)
    spread = jnp.where(lane_d // HEADS - 6 == iota((DOCS, 128), 0), most, 0.0)
    fold = as_bf16(iota((128, SPAN), 0) % HEADS == iota((128, SPAN), 1) % HEADS)
    folded = [
        jnp.dot(piece.astype(jnp.bfloat16), fold, preferred_element_type=jnp.float32)
        for piece in three_parts(spread)
    ]
    maxima_ref[...] = folded[0] + (folded[1] + folded[2])

    whole = tail + (pltpu.roll(tail, 128 - 8, 1) + pltpu.roll(tail, 128 - 16, 1))
    shift = 2 * RING
    far = pltpu.roll(pltpu.roll(whole, 128 - 24, 1), shift, 0)
    share = 1.0 / (1.0 + jnp.exp(far - whole))
    share = jnp.where(row < shift, 1.0, share)
    for h in range(HEADS):
        w = share[:, h : h + 1]
        mine = got_ref[:, h * HD : (h + 1) * HD].astype(jnp.float32)
        other = got_ref[:, WIDE + h * HD : WIDE + (h + 1) * HD].astype(jnp.float32)
        other = pltpu.roll(other, shift, 0)
        out_ref[:, h * HD : (h + 1) * HD] = (mine * w + other * (1.0 - w)).astype(jnp.bfloat16)


VMEM = pl.BlockSpec(memory_space=pltpu.VMEM)
SMEM = pl.BlockSpec(memory_space=pltpu.SMEM)
PARAMS = pltpu.CompilerParams(vmem_limit_bytes=40 * 1024 * 1024)
PREPARE_COST = pl.CostEstimate(flops=10**10, bytes_accessed=10**8, transcendentals=0)


def body(queries, keys, values, doc_lengths, source_row):
    along_ring = [[r * RING + z for z in range(RING)] for r in range(RINGS)]

    def exchange(x, groups):
        return lax.all_to_all(
            x, "ctx", split_axis=0, concat_axis=0, tiled=True, axis_index_groups=groups
        )

    own = jnp.pad(keys, ((0, 0), (0, HD))) + jnp.pad(values, ((0, 0), (HD, 0)))
    before = lax.ppermute(own, "ctx", [(c, c + RING) for c in range(CTX - RING)])
    next_queries = lax.ppermute(queries, "ctx", [(c + RING, c) for c in range(CTX - RING)])
    later = jnp.arange(RING, dtype=jnp.int32) > lax.axis_index("ctx") % RING
    slots = jnp.where(later[:, None, None], own[None], before[None])
    window = exchange(slots, along_ring).reshape(FAR, 2 * HD)
    q_rows, bias, doc = pl.pallas_call(
        prepare_kernel,
        out_shape=(
            jax.ShapeDtypeStruct((PARTS, HEADS * ROWS, HD), jnp.bfloat16),
            jax.ShapeDtypeStruct((PARTS, ROWS, WINDOW), jnp.float32),
            jax.ShapeDtypeStruct((PARTS, ROWS, 128), jnp.int32),
        ),
        in_specs=[SMEM, VMEM, VMEM, VMEM],
        out_specs=(VMEM, VMEM, VMEM),
        compiler_params=PARAMS,
        name="prepare",
    )(doc_lengths, source_row, queries, next_queries)
    wide = PARTS * WIDE + 128
    sent = pl.pallas_call(
        attend_kernel,
        out_shape=jax.ShapeDtypeStruct((ROWS, wide), jnp.bfloat16),
        in_specs=[VMEM, VMEM, VMEM, VMEM, VMEM],
        out_specs=VMEM,
        compiler_params=PARAMS,
        name="attend",
    )(q_rows, bias, doc, window, own)
    got = lax.all_to_all(
        sent.reshape(CTX, 2, wide), "ctx", split_axis=0, concat_axis=0, tiled=True
    )
    context, maxima = pl.pallas_call(
        merge_kernel,
        out_shape=(
            jax.ShapeDtypeStruct((ROWS, WIDE), jnp.bfloat16),
            jax.ShapeDtypeStruct((DOCS, SPAN), jnp.float32),
        ),
        in_specs=[VMEM],
        out_specs=(VMEM, VMEM),
        compiler_params=PARAMS,
        name="merge",
    )(got.reshape(ROWS, wide))
    head = lax.axis_index("head")
    owner = lax.broadcasted_iota(jnp.int32, (DOCS, SPAN), 1) // HEADS
    everyone = maxima
    for k in range(1, GROUPS):
        moved = lax.ppermute(maxima, "head", [(i, (i + k) % GROUPS) for i in range(GROUPS)])
        everyone = jnp.where(owner == (head + GROUPS - k) % GROUPS, moved, everyone)
    return (context, everyone.T)


def solution(mesh):
    return jax.shard_map(
        body,
        mesh=mesh,
        in_specs=(P("ctx", "head"), P("ctx", "head"), P("ctx", "head"), P(), P()),
        out_specs=(P("ctx", "head"), P()),
        check_vma=False,
    )
```

```python
import math

import jax
import jax.numpy as jnp
from jax import lax
from jax.experimental import pallas as pl
from jax.experimental.pallas import tpu as pltpu
from jax.sharding import PartitionSpec as P

HD = 128
HEADS = 8
GROUPS = 4
DOCS = 8
ROWS = 128
RING = 8
RINGS = 8
CTX = RING * RINGS
PARTS = 2
WIDE = HEADS * HD
FAR = RING * ROWS
WINDOW = FAR + ROWS
NEG_BIG = -1e30
SCALE = 1.0 / math.sqrt(HD)
SCALE_LOG2E = SCALE * math.log2(math.e)
HEADS_AT_ONCE = 4
SPAN = GROUPS * HEADS


def dot_nt(a, b):
    return lax.dot_general(a, b, (((1,), (1,)), ((), ())), preferred_element_type=jnp.float32)


def as_bf16(mask):
    return mask.astype(jnp.float32).astype(jnp.bfloat16)


def three_parts(x):
    first = x.astype(jnp.bfloat16).astype(jnp.float32)
    second = (x - first).astype(jnp.bfloat16).astype(jnp.float32)
    return first, second, x - first - second


def iota(shape, dim):
    return lax.broadcasted_iota(jnp.int32, shape, dim)


def prepare_kernel(
    lengths_ref, source_ref, q0_ref, q1_ref, q_out, bias_out, doc_out
):
    me = lax.axis_index("ctx")
    lane = iota((ROWS, 128), 1)
    row = iota((ROWS, 128), 0)
    local = as_bf16(source_ref[...] - iota((CTX, 128), 1) // 2 * ROWS)
    spread = as_bf16(iota((ROWS, CTX), 0) // 2 == iota((ROWS, CTX), 1))
    table = jnp.dot(spread, local, preferred_element_type=jnp.float32)
    in_ring = me % RING
    base = me - in_ring
    for part, rows_ref in enumerate((q0_ref, q1_ref)):
        chunk = me + RING * part
        pick = jnp.sum(
            jnp.where(lane == 2 * chunk + row % 2, table, 0.0), axis=1, keepdims=True
        ).astype(jnp.int32)
        q_all = jnp.dot(as_bf16(lane == pick), rows_ref[...], preferred_element_type=jnp.float32)
        for h in range(HEADS):
            q_out[part, h * ROWS : (h + 1) * ROWS, :] = q_all[:, h * HD : (h + 1) * HD].astype(
                jnp.bfloat16
            )
        pos = chunk * ROWS + pick
        start = jnp.zeros_like(pos)
        doc = jnp.zeros_like(pos)
        end = jnp.int32(0)
        for i in range(DOCS):
            end = end + lengths_ref[i]
            passed = pos >= end
            start = jnp.where(passed, end, start)
            doc = doc + passed.astype(jnp.int32)
        doc_out[part] = jnp.broadcast_to(doc, (ROWS, 128))
        for j in range(RING + part):
            if j == RING:
                block = me
            else:
                block = base + j - jnp.where(j + part > in_ring, RING, 0)
            key_pos = block * ROWS + lane
            ok = (key_pos >= start) & (key_pos <= pos)
            bias_out[part, :, j * 128 : (j + 1) * 128] = jnp.where(ok, 0.0, NEG_BIG)


def attend_kernel(q_ref, bias_ref, doc_ref, kv_ref, own_ref, out_ref, kv_scr):
    lane = iota((ROWS, 128), 1)
    n = HEADS_AT_ONCE
    kv_scr[...] = kv_ref[...]
    kv_scr[pl.ds(pl.multiple_of(lax.axis_index("ctx") % RING * ROWS, ROWS), ROWS), :] = own_ref[...]
    all_logs = []
    best = jnp.full((ROWS, 128), NEG_BIG, jnp.float32)
    for part in range(PARTS):
        peaks = jnp.full((ROWS, 128), NEG_BIG, jnp.float32)
        logs = jnp.full((ROWS, 128), NEG_BIG, jnp.float32)
        sources = [(kv_scr, 0, FAR)] if part == 0 else [(kv_ref, 0, FAR), (own_ref, FAR, WINDOW)]
        for h0 in range(0, HEADS, n):
            q = q_ref[part, h0 * ROWS : (h0 + n) * ROWS, :]
            scores = [
                dot_nt(q, ref[:, :HD]).reshape(n, ROWS, high - low)
                + bias_ref[part, :, low:high][None]
                for ref, low, high in sources
            ]
            tops = [jnp.max(s, axis=2, keepdims=True) for s in scores]
            top = tops[0] if part == 0 else jnp.maximum(tops[0], tops[1])
            weights = [jnp.exp2((s - top) * SCALE_LOG2E) for s in scores]
            total = sum(jnp.sum(w, axis=2, keepdims=True) for w in weights)
            acc = sum(
                jnp.dot(
                    w.astype(jnp.bfloat16).reshape(n * ROWS, high - low),
                    ref[:, HD:],
                    preferred_element_type=jnp.float32,
                )
                for w, (ref, low, high) in zip(weights, sources)
            )
            context = acc.reshape(n, ROWS, HD) / total
            for k in range(n):
                h = h0 + k
                at = part * WIDE + h * HD
                out_ref[:, at : at + HD] = context[k].astype(jnp.bfloat16)
                peak = top[k] * SCALE
                peaks = jnp.where(lane % 8 == h, peak, peaks)
                logs = jnp.where(lane % 8 == h, peak + jnp.log(total[k]), logs)
        all_logs.append(logs)
        best = jnp.maximum(best, jnp.where(lane // 8 == doc_ref[part], peaks, NEG_BIG))

    logs = jnp.where(lane < 24, all_logs[0], all_logs[1])
    step = lane % 24 // 8
    pieces = three_parts(logs)
    tail = jnp.where(step == 0, pieces[0], jnp.where(step == 1, pieces[1], pieces[2]))
    most = three_parts(pltpu.roll(jnp.max(best, axis=0, keepdims=True), 48, 1))
    maxima = jnp.where(iota((ROWS, 128), 0) % 2 == 0, most[0], most[1])
    tail = jnp.where(lane < 48, tail, jnp.where(lane < 112, maxima, 0.0))
    out_ref[:, PARTS * WIDE :] = tail.astype(jnp.bfloat16)


def maxima_kernel(tail_ref, maxima_ref):
    row = iota((ROWS, 128), 0)
    tail = tail_ref[:, PARTS * WIDE :].astype(jnp.float32)

    most = tail + pltpu.roll(tail, ROWS - 1, 0)
    most = jnp.max(jnp.where(row % 2 == 0, most, NEG_BIG), axis=0, keepdims=True)
    lane_d = iota((DOCS, 128), 1)
    spread = jnp.where(lane_d // HEADS - 6 == iota((DOCS, 128), 0), most, 0.0)
    fold = as_bf16(iota((128, SPAN), 0) % HEADS == iota((128, SPAN), 1) % HEADS)
    folded = [
        jnp.dot(piece.astype(jnp.bfloat16), fold, preferred_element_type=jnp.float32)
        for piece in three_parts(spread)
    ]
    mine = iota((DOCS, SPAN), 1) // HEADS == lax.axis_index("head")
    maxima_ref[...] = jnp.where(mine, folded[0] + (folded[1] + folded[2]), 0.0)


def merge_kernel(got_ref, out_ref):
    row = iota((ROWS, 128), 0)
    tail = got_ref[:, PARTS * WIDE :].astype(jnp.float32)

    whole = tail + (pltpu.roll(tail, 128 - 8, 1) + pltpu.roll(tail, 128 - 16, 1))
    shift = 2 * RING
    far = pltpu.roll(pltpu.roll(whole, 128 - 24, 1), shift, 0)
    share = 1.0 / (1.0 + jnp.exp(far - whole))
    share = jnp.where(row < shift, 1.0, share)
    for h in range(HEADS):
        w = share[:, h : h + 1]
        mine = got_ref[:, h * HD : (h + 1) * HD].astype(jnp.float32)
        other = got_ref[:, WIDE + h * HD : WIDE + (h + 1) * HD].astype(jnp.float32)
        other = pltpu.roll(other, shift, 0)
        out_ref[:, h * HD : (h + 1) * HD] = (mine * w + other * (1.0 - w)).astype(jnp.bfloat16)


VMEM = pl.BlockSpec(memory_space=pltpu.VMEM)
SMEM = pl.BlockSpec(memory_space=pltpu.SMEM)
PARAMS = pltpu.CompilerParams(vmem_limit_bytes=40 * 1024 * 1024)
MERGE_COST = pl.CostEstimate(flops=10**8, bytes_accessed=10**7, transcendentals=0)


def body(queries, keys, values, doc_lengths, source_row):
    along_ring = [[r * RING + z for z in range(RING)] for r in range(RINGS)]

    def exchange(x, groups):
        return lax.all_to_all(
            x, "ctx", split_axis=0, concat_axis=0, tiled=True, axis_index_groups=groups
        )

    own = jnp.pad(keys, ((0, 0), (0, HD))) + jnp.pad(values, ((0, 0), (HD, 0)))
    before = lax.ppermute(own, "ctx", [(c, c + RING) for c in range(CTX - RING)])
    next_queries = lax.ppermute(queries, "ctx", [(c + RING, c) for c in range(CTX - RING)])
    later = jnp.arange(RING, dtype=jnp.int32) > lax.axis_index("ctx") % RING
    slots = jnp.where(later[:, None, None], own[None], before[None])
    window = exchange(slots, along_ring).reshape(FAR, 2 * HD)
    q_rows, bias, doc = pl.pallas_call(
        prepare_kernel,
        out_shape=(
            jax.ShapeDtypeStruct((PARTS, HEADS * ROWS, HD), jnp.bfloat16),
            jax.ShapeDtypeStruct((PARTS, ROWS, WINDOW), jnp.float32),
            jax.ShapeDtypeStruct((PARTS, ROWS, 128), jnp.int32),
        ),
        in_specs=[SMEM, VMEM, VMEM, VMEM],
        out_specs=(VMEM, VMEM, VMEM),
        compiler_params=PARAMS,
        name="prepare",
    )(doc_lengths, source_row, queries, next_queries)
    wide = PARTS * WIDE + 128
    sent = pl.pallas_call(
        attend_kernel,
        out_shape=jax.ShapeDtypeStruct((ROWS, wide), jnp.bfloat16),
        in_specs=[VMEM, VMEM, VMEM, VMEM, VMEM],
        out_specs=VMEM,
        scratch_shapes=[pltpu.VMEM((FAR, 2 * HD), jnp.bfloat16)],
        compiler_params=PARAMS,
        name="attend",
    )(q_rows, bias, doc, window, own)
    got = lax.all_to_all(
        sent.reshape(CTX, 2, wide), "ctx", split_axis=0, concat_axis=0, tiled=True
    )
    got = got.reshape(ROWS, wide)
    maxima = pl.pallas_call(
        maxima_kernel,
        out_shape=jax.ShapeDtypeStruct((DOCS, SPAN), jnp.float32),
        in_specs=[VMEM],
        out_specs=VMEM,
        compiler_params=PARAMS,
        name="maxima",
    )(got)
    everyone = maxima
    for k in range(1, GROUPS):
        everyone = everyone + lax.ppermute(
            maxima, "head", [(i, (i + k) % GROUPS) for i in range(GROUPS)]
        )
    context = pl.pallas_call(
        merge_kernel,
        out_shape=jax.ShapeDtypeStruct((ROWS, WIDE), jnp.bfloat16),
        in_specs=[VMEM],
        out_specs=VMEM,
        cost_estimate=MERGE_COST,
        compiler_params=PARAMS,
        name="merge",
    )(got)
    return (context, everyone.T)


def solution(mesh):
    return jax.shard_map(
        body,
        mesh=mesh,
        in_specs=(P("ctx", "head"), P("ctx", "head"), P("ctx", "head"), P(), P()),
        out_specs=(P("ctx", "head"), P()),
        check_vma=False,
    )
```

```python
import math

import jax
import jax.numpy as jnp
from jax import lax
from jax.experimental import pallas as pl
from jax.experimental.pallas import tpu as pltpu
from jax.sharding import PartitionSpec as P

HD = 128
HEADS = 8
GROUPS = 4
DOCS = 8
ROWS = 128
RING = 8
RINGS = 8
CTX = RING * RINGS
PARTS = 2
WIDE = HEADS * HD
FAR = RING * ROWS
WINDOW = FAR + ROWS
NEG_BIG = -1e30
SCALE = 1.0 / math.sqrt(HD)
SCALE_LOG2E = SCALE * math.log2(math.e)
HEADS_AT_ONCE = 2
SPAN = GROUPS * HEADS


def dot_nt(a, b):
    return lax.dot_general(a, b, (((1,), (1,)), ((), ())), preferred_element_type=jnp.float32)


def as_bf16(mask):
    return mask.astype(jnp.float32).astype(jnp.bfloat16)


def three_parts(x):
    first = x.astype(jnp.bfloat16).astype(jnp.float32)
    second = (x - first).astype(jnp.bfloat16).astype(jnp.float32)
    return first, second, x - first - second


def iota(shape, dim):
    return lax.broadcasted_iota(jnp.int32, shape, dim)


def prepare_kernel(
    lengths_ref, source_ref, q0_ref, q1_ref, q_out, bias_out, doc_out
):
    me = lax.axis_index("ctx")
    lane = iota((ROWS, 128), 1)
    row = iota((ROWS, 128), 0)
    local = as_bf16(source_ref[...] - iota((CTX, 128), 1) // 2 * ROWS)
    spread = as_bf16(iota((ROWS, CTX), 0) // 2 == iota((ROWS, CTX), 1))
    table = jnp.dot(spread, local, preferred_element_type=jnp.float32)
    in_ring = me % RING
    base = me - in_ring
    for part, rows_ref in enumerate((q0_ref, q1_ref)):
        chunk = me + RING * part
        pick = jnp.sum(
            jnp.where(lane == 2 * chunk + row % 2, table, 0.0), axis=1, keepdims=True
        ).astype(jnp.int32)
        q_all = jnp.dot(as_bf16(lane == pick), rows_ref[...], preferred_element_type=jnp.float32)
        for h in range(HEADS):
            q_out[part, h * ROWS : (h + 1) * ROWS, :] = q_all[:, h * HD : (h + 1) * HD].astype(
                jnp.bfloat16
            )
        pos = chunk * ROWS + pick
        start = jnp.zeros_like(pos)
        doc = jnp.zeros_like(pos)
        end = jnp.int32(0)
        for i in range(DOCS):
            end = end + lengths_ref[i]
            passed = pos >= end
            start = jnp.where(passed, end, start)
            doc = doc + passed.astype(jnp.int32)
        doc_out[part] = jnp.broadcast_to(doc, (ROWS, 128))
        for j in range(RING + part):
            if j == RING:
                block = me
            else:
                block = base + j - jnp.where(j + part > in_ring, RING, 0)
            key_pos = block * ROWS + lane
            ok = (key_pos >= start) & (key_pos <= pos)
            bias_out[part, :, j * 128 : (j + 1) * 128] = jnp.where(ok, 0.0, NEG_BIG)


def attend_kernel(q_ref, bias_ref, doc_ref, kv_ref, own_ref, out_ref, kv_scr):
    lane = iota((ROWS, 128), 1)
    n = HEADS_AT_ONCE
    kv_scr[...] = kv_ref[...]
    kv_scr[pl.ds(pl.multiple_of(lax.axis_index("ctx") % RING * ROWS, ROWS), ROWS), :] = own_ref[...]
    all_peaks = [jnp.full((ROWS, 128), NEG_BIG, jnp.float32)] * PARTS
    all_logs = [jnp.full((ROWS, 128), NEG_BIG, jnp.float32)] * PARTS
    sources = [[(kv_scr, 0, FAR)], [(kv_ref, 0, FAR), (own_ref, FAR, WINDOW)]]

    def scores_of(part, h0):
        q = q_ref[part, h0 * ROWS : (h0 + n) * ROWS, :]
        return [
            dot_nt(q, ref[:, :HD]).reshape(n, ROWS, high - low) + bias_ref[part, :, low:high][None]
            for ref, low, high in sources[part]
        ]

    jobs = [(part, h0) for part in range(PARTS) for h0 in range(0, HEADS, n)]
    ahead = scores_of(*jobs[0])
    for i, (part, h0) in enumerate(jobs):
        scores = ahead
        if i + 1 < len(jobs):
            ahead = scores_of(*jobs[i + 1])
        tops = [jnp.max(s, axis=2, keepdims=True) for s in scores]
        top = tops[0] if part == 0 else jnp.maximum(tops[0], tops[1])
        weights = [jnp.exp2((s - top) * SCALE_LOG2E) for s in scores]
        total = sum(jnp.sum(w, axis=2, keepdims=True) for w in weights)
        acc = sum(
            jnp.dot(
                w.astype(jnp.bfloat16).reshape(n * ROWS, high - low),
                ref[:, HD:],
                preferred_element_type=jnp.float32,
            )
            for w, (ref, low, high) in zip(weights, sources[part])
        )
        context = acc.reshape(n, ROWS, HD) * (1.0 / total)
        for k in range(n):
            h = h0 + k
            at = part * WIDE + h * HD
            out_ref[:, at : at + HD] = context[k].astype(jnp.bfloat16)
            peak = top[k] * SCALE
            all_peaks[part] = jnp.where(lane % 8 == h, peak, all_peaks[part])
            all_logs[part] = jnp.where(lane % 8 == h, peak + jnp.log(total[k]), all_logs[part])
    best = jnp.full((ROWS, 128), NEG_BIG, jnp.float32)
    for part in range(PARTS):
        best = jnp.maximum(best, jnp.where(lane // 8 == doc_ref[part], all_peaks[part], NEG_BIG))

    logs = jnp.where(lane < 24, all_logs[0], all_logs[1])
    step = lane % 24 // 8
    pieces = three_parts(logs)
    tail = jnp.where(step == 0, pieces[0], jnp.where(step == 1, pieces[1], pieces[2]))
    most = three_parts(pltpu.roll(jnp.max(best, axis=0, keepdims=True), 48, 1))
    maxima = jnp.where(iota((ROWS, 128), 0) % 2 == 0, most[0], most[1])
    tail = jnp.where(lane < 48, tail, jnp.where(lane < 112, maxima, 0.0))
    out_ref[:, PARTS * WIDE :] = tail.astype(jnp.bfloat16)


def maxima_kernel(tail_ref, maxima_ref):
    row = iota((ROWS, 128), 0)
    tail = tail_ref[:, PARTS * WIDE :].astype(jnp.float32)

    most = tail + pltpu.roll(tail, ROWS - 1, 0)
    most = jnp.max(jnp.where(row % 2 == 0, most, NEG_BIG), axis=0, keepdims=True)
    lane_d = iota((DOCS, 128), 1)
    spread = jnp.where(lane_d // HEADS - 6 == iota((DOCS, 128), 0), most, 0.0)
    fold = as_bf16(iota((128, SPAN), 0) % HEADS == iota((128, SPAN), 1) % HEADS)
    folded = [
        jnp.dot(piece.astype(jnp.bfloat16), fold, preferred_element_type=jnp.float32)
        for piece in three_parts(spread)
    ]
    mine = iota((DOCS, SPAN), 1) // HEADS == lax.axis_index("head")
    maxima_ref[...] = jnp.where(mine, folded[0] + (folded[1] + folded[2]), 0.0)


def merge_kernel(got_ref, out_ref):
    row = iota((ROWS, 128), 0)
    tail = got_ref[:, PARTS * WIDE :].astype(jnp.float32)

    whole = tail + (pltpu.roll(tail, 128 - 8, 1) + pltpu.roll(tail, 128 - 16, 1))
    shift = 2 * RING
    far = pltpu.roll(pltpu.roll(whole, 128 - 24, 1), shift, 0)
    share = 1.0 / (1.0 + jnp.exp(far - whole))
    share = jnp.where(row < shift, 1.0, share)
    for h in range(HEADS):
        w = share[:, h : h + 1]
        mine = got_ref[:, h * HD : (h + 1) * HD].astype(jnp.float32)
        other = got_ref[:, WIDE + h * HD : WIDE + (h + 1) * HD].astype(jnp.float32)
        other = pltpu.roll(other, shift, 0)
        out_ref[:, h * HD : (h + 1) * HD] = (mine * w + other * (1.0 - w)).astype(jnp.bfloat16)


VMEM = pl.BlockSpec(memory_space=pltpu.VMEM)
SMEM = pl.BlockSpec(memory_space=pltpu.SMEM)
PARAMS = pltpu.CompilerParams(vmem_limit_bytes=40 * 1024 * 1024)
MERGE_COST = pl.CostEstimate(flops=10**8, bytes_accessed=10**7, transcendentals=0)


def body(queries, keys, values, doc_lengths, source_row):
    along_ring = [[r * RING + z for z in range(RING)] for r in range(RINGS)]

    def exchange(x, groups):
        return lax.all_to_all(
            x, "ctx", split_axis=0, concat_axis=0, tiled=True, axis_index_groups=groups
        )

    own = jnp.pad(keys, ((0, 0), (0, HD))) + jnp.pad(values, ((0, 0), (HD, 0)))
    before = lax.ppermute(own, "ctx", [(c, c + RING) for c in range(CTX - RING)])
    next_queries = lax.ppermute(queries, "ctx", [(c + RING, c) for c in range(CTX - RING)])
    later = jnp.arange(RING, dtype=jnp.int32) > lax.axis_index("ctx") % RING
    slots = jnp.where(later[:, None, None], own[None], before[None])
    window = exchange(slots, along_ring).reshape(FAR, 2 * HD)
    q_rows, bias, doc = pl.pallas_call(
        prepare_kernel,
        out_shape=(
            jax.ShapeDtypeStruct((PARTS, HEADS * ROWS, HD), jnp.bfloat16),
            jax.ShapeDtypeStruct((PARTS, ROWS, WINDOW), jnp.float32),
            jax.ShapeDtypeStruct((PARTS, ROWS, 128), jnp.int32),
        ),
        in_specs=[SMEM, VMEM, VMEM, VMEM],
        out_specs=(VMEM, VMEM, VMEM),
        compiler_params=PARAMS,
        name="prepare",
    )(doc_lengths, source_row, queries, next_queries)
    wide = PARTS * WIDE + 128
    sent = pl.pallas_call(
        attend_kernel,
        out_shape=jax.ShapeDtypeStruct((ROWS, wide), jnp.bfloat16),
        in_specs=[VMEM, VMEM, VMEM, VMEM, VMEM],
        out_specs=VMEM,
        scratch_shapes=[pltpu.VMEM((FAR, 2 * HD), jnp.bfloat16)],
        compiler_params=PARAMS,
        name="attend",
    )(q_rows, bias, doc, window, own)
    got = lax.all_to_all(
        sent.reshape(CTX, 2, wide), "ctx", split_axis=0, concat_axis=0, tiled=True
    )
    got = got.reshape(ROWS, wide)
    maxima = pl.pallas_call(
        maxima_kernel,
        out_shape=jax.ShapeDtypeStruct((DOCS, SPAN), jnp.float32),
        in_specs=[VMEM],
        out_specs=VMEM,
        compiler_params=PARAMS,
        name="maxima",
    )(got)
    everyone = maxima
    for k in range(1, GROUPS):
        everyone = everyone + lax.ppermute(
            maxima, "head", [(i, (i + k) % GROUPS) for i in range(GROUPS)]
        )
    context = pl.pallas_call(
        merge_kernel,
        out_shape=jax.ShapeDtypeStruct((ROWS, WIDE), jnp.bfloat16),
        in_specs=[VMEM],
        out_specs=VMEM,
        cost_estimate=MERGE_COST,
        compiler_params=PARAMS,
        name="merge",
    )(got)
    return (context, everyone.T)


def solution(mesh):
    return jax.shard_map(
        body,
        mesh=mesh,
        in_specs=(P("ctx", "head"), P("ctx", "head"), P("ctx", "head"), P(), P()),
        out_specs=(P("ctx", "head"), P()),
        check_vma=False,
    )
```

```python
import math

import jax
import jax.numpy as jnp
from jax import lax
from jax.experimental import pallas as pl
from jax.experimental.pallas import tpu as pltpu
from jax.sharding import PartitionSpec as P

HD = 128
HEADS = 8
GROUPS = 4
DOCS = 8
ROWS = 128
RING = 8
RINGS = 8
CTX = RING * RINGS
PARTS = 2
WIDE = HEADS * HD
FAR = RING * ROWS
WINDOW = FAR + ROWS
NEG_BIG = -1e30
SCALE = 1.0 / math.sqrt(HD)
SCALE_LOG2E = SCALE * math.log2(math.e)
HEADS_AT_ONCE = 2
ORDER = tuple(range(RINGS))
SPAN = GROUPS * HEADS


def dot_nt(a, b):
    return lax.dot_general(a, b, (((1,), (1,)), ((), ())), preferred_element_type=jnp.float32)


def as_bf16(mask):
    return mask.astype(jnp.float32).astype(jnp.bfloat16)


def three_parts(x):
    first = x.astype(jnp.bfloat16).astype(jnp.float32)
    second = (x - first).astype(jnp.bfloat16).astype(jnp.float32)
    return first, second, x - first - second


def iota(shape, dim):
    return lax.broadcasted_iota(jnp.int32, shape, dim)


def device_at(place):
    return place % RINGS * RING + place // RINGS


def prepare_kernel(
    lengths_ref, source_ref, q0_ref, q1_ref, q_out, bias_out, doc_out
):
    me = lax.axis_index("ctx")
    lane = iota((ROWS, 128), 1)
    row = iota((ROWS, 128), 0)
    local = as_bf16(source_ref[...] - iota((CTX, 128), 1) // 2 * ROWS)
    spread = as_bf16(device_at(iota((ROWS, CTX), 0) // 2) == iota((ROWS, CTX), 1))
    table = jnp.dot(spread, local, preferred_element_type=jnp.float32)
    in_ring = me % RING
    base = me - in_ring
    for part, rows_ref in enumerate((q0_ref, q1_ref)):
        chunk = me + RING * part
        pick = jnp.sum(
            jnp.where(lane == 2 * chunk + row % 2, table, 0.0), axis=1, keepdims=True
        ).astype(jnp.int32)
        q_all = jnp.dot(as_bf16(lane == pick), rows_ref[...], preferred_element_type=jnp.float32)
        for h in range(HEADS):
            q_out[part, h * ROWS : (h + 1) * ROWS, :] = q_all[:, h * HD : (h + 1) * HD].astype(
                jnp.bfloat16
            )
        pos = chunk * ROWS + pick
        start = jnp.zeros_like(pos)
        doc = jnp.zeros_like(pos)
        end = jnp.int32(0)
        for i in range(DOCS):
            end = end + lengths_ref[i]
            passed = pos >= end
            start = jnp.where(passed, end, start)
            doc = doc + passed.astype(jnp.int32)
        doc_out[part] = jnp.broadcast_to(doc, (ROWS, 128))
        for j in range(RING + part):
            if j == RING:
                block = me
            else:
                block = base + j - jnp.where(j + part > in_ring, RING, 0)
            key_pos = block * ROWS + lane
            ok = (key_pos >= start) & (key_pos <= pos)
            bias_out[part, :, j * 128 : (j + 1) * 128] = jnp.where(ok, 0.0, NEG_BIG)


def attend_kernel(q_ref, bias_ref, doc_ref, kv_ref, own_ref, out_ref, kv_scr):
    lane = iota((ROWS, 128), 1)
    n = HEADS_AT_ONCE
    kv_scr[...] = kv_ref[...]
    kv_scr[pl.ds(pl.multiple_of(lax.axis_index("ctx") % RING * ROWS, ROWS), ROWS), :] = own_ref[...]
    all_peaks = [jnp.full((ROWS, 128), NEG_BIG, jnp.float32)] * PARTS
    all_logs = [jnp.full((ROWS, 128), NEG_BIG, jnp.float32)] * PARTS
    sources = [[(kv_scr, 0, FAR)], [(kv_ref, 0, FAR), (own_ref, FAR, WINDOW)]]

    def scores_of(part, h0):
        q = q_ref[part, h0 * ROWS : (h0 + n) * ROWS, :]
        return [
            dot_nt(q, ref[:, :HD]).reshape(n, ROWS, high - low) + bias_ref[part, :, low:high][None]
            for ref, low, high in sources[part]
        ]

    jobs = [(part, h0) for part in range(PARTS) for h0 in range(0, HEADS, n)]
    ahead = scores_of(*jobs[0])
    for i, (part, h0) in enumerate(jobs):
        scores = ahead
        if i + 1 < len(jobs):
            ahead = scores_of(*jobs[i + 1])
        tops = [jnp.max(s, axis=2, keepdims=True) for s in scores]
        top = tops[0] if part == 0 else jnp.maximum(tops[0], tops[1])
        weights = [jnp.exp2((s - top) * SCALE_LOG2E) for s in scores]
        total = sum(jnp.sum(w, axis=2, keepdims=True) for w in weights)
        acc = sum(
            jnp.dot(
                w.astype(jnp.bfloat16).reshape(n * ROWS, high - low),
                ref[:, HD:],
                preferred_element_type=jnp.float32,
            )
            for w, (ref, low, high) in zip(weights, sources[part])
        )
        context = acc.reshape(n, ROWS, HD) * (1.0 / total)
        for k in range(n):
            h = h0 + k
            at = part * WIDE + h * HD
            out_ref[:, at : at + HD] = context[k].astype(jnp.bfloat16)
            peak = top[k] * SCALE
            all_peaks[part] = jnp.where(lane % 8 == h, peak, all_peaks[part])
            all_logs[part] = jnp.where(lane % 8 == h, peak + jnp.log(total[k]), all_logs[part])
    best = jnp.full((ROWS, 128), NEG_BIG, jnp.float32)
    for part in range(PARTS):
        best = jnp.maximum(best, jnp.where(lane // 8 == doc_ref[part], all_peaks[part], NEG_BIG))

    logs = jnp.where(lane < 24, all_logs[0], all_logs[1])
    step = lane % 24 // 8
    pieces = three_parts(logs)
    tail = jnp.where(step == 0, pieces[0], jnp.where(step == 1, pieces[1], pieces[2]))
    most = three_parts(pltpu.roll(jnp.max(best, axis=0, keepdims=True), 48, 1))
    maxima = jnp.where(iota((ROWS, 128), 0) % 2 == 0, most[0], most[1])
    tail = jnp.where(lane < 48, tail, jnp.where(lane < 112, maxima, 0.0))
    out_ref[:, PARTS * WIDE :] = tail.astype(jnp.bfloat16)


def maxima_kernel(tail_ref, maxima_ref):
    row = iota((ROWS, 128), 0)
    tail = tail_ref[:, PARTS * WIDE :].astype(jnp.float32)

    most = tail + pltpu.roll(tail, ROWS - 1, 0)
    most = jnp.max(jnp.where(row % 2 == 0, most, NEG_BIG), axis=0, keepdims=True)
    lane_d = iota((DOCS, 128), 1)
    spread = jnp.where(lane_d // HEADS - 6 == iota((DOCS, 128), 0), most, 0.0)
    fold = as_bf16(iota((128, SPAN), 0) % HEADS == iota((128, SPAN), 1) % HEADS)
    folded = [
        jnp.dot(piece.astype(jnp.bfloat16), fold, preferred_element_type=jnp.float32)
        for piece in three_parts(spread)
    ]
    mine = iota((DOCS, SPAN), 1) // HEADS == lax.axis_index("head")
    maxima_ref[...] = jnp.where(mine, folded[0] + (folded[1] + folded[2]), 0.0)


def merge_kernel(got_ref, out_ref):
    row = iota((ROWS, 128), 0)

    to = iota((ROWS, ROWS), 0)
    source = to // 2 % RING * 2 * RINGS + to // (2 * RING) * 2 + to % 2
    from_near = as_bf16(iota((ROWS, ROWS), 1) == source)
    from_far = as_bf16(iota((ROWS, ROWS), 1) == source - 2)
    whole = jnp.concatenate([got_ref[:, :WIDE], got_ref[:, PARTS * WIDE :]], axis=1)
    near = jnp.dot(from_near, whole, preferred_element_type=jnp.float32)
    whole = jnp.concatenate([got_ref[:, WIDE : PARTS * WIDE], got_ref[:, PARTS * WIDE :]], axis=1)
    far = jnp.dot(from_far, whole, preferred_element_type=jnp.float32)

    def summed(tail):
        return tail + (pltpu.roll(tail, 128 - 8, 1) + pltpu.roll(tail, 128 - 16, 1))

    log_far = pltpu.roll(summed(far[:, WIDE:]), 128 - 24, 1)
    share = 1.0 / (1.0 + jnp.exp(log_far - summed(near[:, WIDE:])))
    share = jnp.where(row < 2 * RING, 1.0, share)
    for h in range(HEADS):
        w = share[:, h : h + 1]
        at = slice(h * HD, (h + 1) * HD)
        out_ref[:, at] = (near[:, at] * w + far[:, at] * (1.0 - w)).astype(jnp.bfloat16)


VMEM = pl.BlockSpec(memory_space=pltpu.VMEM)
SMEM = pl.BlockSpec(memory_space=pltpu.SMEM)
PARAMS = pltpu.CompilerParams(vmem_limit_bytes=40 * 1024 * 1024)
MERGE_COST = pl.CostEstimate(flops=10**8, bytes_accessed=10**7, transcendentals=0)


def body(queries, keys, values, doc_lengths, source_row):
    along_ring = [[r * RING + z for z in range(RING)] for r in range(RINGS)]

    def exchange(x, groups):
        return lax.all_to_all(
            x, "ctx", split_axis=0, concat_axis=0, tiled=True, axis_index_groups=groups
        )

    own = jnp.pad(keys, ((0, 0), (0, HD))) + jnp.pad(values, ((0, 0), (HD, 0)))
    before = lax.ppermute(own, "ctx", [(c, c + RING) for c in range(CTX - RING)])
    next_queries = lax.ppermute(queries, "ctx", [(c + RING, c) for c in range(CTX - RING)])
    later = jnp.arange(RING, dtype=jnp.int32) > lax.axis_index("ctx") % RING
    slots = jnp.where(later[:, None, None], own[None], before[None])
    window = exchange(slots, along_ring).reshape(FAR, 2 * HD)
    q_rows, bias, doc = pl.pallas_call(
        prepare_kernel,
        out_shape=(
            jax.ShapeDtypeStruct((PARTS, HEADS * ROWS, HD), jnp.bfloat16),
            jax.ShapeDtypeStruct((PARTS, ROWS, WINDOW), jnp.float32),
            jax.ShapeDtypeStruct((PARTS, ROWS, 128), jnp.int32),
        ),
        in_specs=[SMEM, VMEM, VMEM, VMEM],
        out_specs=(VMEM, VMEM, VMEM),
        compiler_params=PARAMS,
        name="prepare",
    )(doc_lengths, source_row, queries, next_queries)
    wide = PARTS * WIDE + 128
    sent = pl.pallas_call(
        attend_kernel,
        out_shape=jax.ShapeDtypeStruct((ROWS, wide), jnp.bfloat16),
        in_specs=[VMEM, VMEM, VMEM, VMEM, VMEM],
        out_specs=VMEM,
        scratch_shapes=[pltpu.VMEM((FAR, 2 * HD), jnp.bfloat16)],
        compiler_params=PARAMS,
        name="attend",
    )(q_rows, bias, doc, window, own)
    got = lax.all_to_all(
        sent.reshape(CTX, 2, wide),
        "ctx",
        split_axis=0,
        concat_axis=0,
        tiled=True,
        axis_index_groups=[[r * RING + z for z in range(RING) for r in ORDER]],
    )
    got = got.reshape(ROWS, wide)
    maxima = pl.pallas_call(
        maxima_kernel,
        out_shape=jax.ShapeDtypeStruct((DOCS, SPAN), jnp.float32),
        in_specs=[VMEM],
        out_specs=VMEM,
        compiler_params=PARAMS,
        name="maxima",
    )(got)
    everyone = maxima
    for k in range(1, GROUPS):
        everyone = everyone + lax.ppermute(
            maxima, "head", [(i, (i + k) % GROUPS) for i in range(GROUPS)]
        )
    context = pl.pallas_call(
        merge_kernel,
        out_shape=jax.ShapeDtypeStruct((ROWS, WIDE), jnp.bfloat16),
        in_specs=[VMEM],
        out_specs=VMEM,
        cost_estimate=MERGE_COST,
        compiler_params=PARAMS,
        name="merge",
    )(got)
    return (context, everyone.T)


def solution(mesh):
    return jax.shard_map(
        body,
        mesh=mesh,
        in_specs=(P("ctx", "head"), P("ctx", "head"), P("ctx", "head"), P(), P()),
        out_specs=(P("ctx", "head"), P()),
        check_vma=False,
    )
```

```python
import math

import jax
import jax.numpy as jnp
from jax import lax
from jax.experimental import pallas as pl
from jax.experimental.pallas import tpu as pltpu
from jax.sharding import PartitionSpec as P

HD = 128
HEADS = 8
GROUPS = 4
DOCS = 8
ROWS = 128
RING = 8
RINGS = 8
CTX = RING * RINGS
PARTS = 2
WIDE = HEADS * HD
FAR = RING * ROWS
WINDOW = FAR + ROWS
NEG_BIG = -1e30
SCALE = 1.0 / math.sqrt(HD)
SCALE_LOG2E = SCALE * math.log2(math.e)
HEADS_AT_ONCE = 2
ORDER = tuple(range(RINGS))
SPAN = GROUPS * HEADS


def dot_nt(a, b):
    return lax.dot_general(a, b, (((1,), (1,)), ((), ())), preferred_element_type=jnp.float32)


def as_bf16(mask):
    return mask.astype(jnp.float32).astype(jnp.bfloat16)


def three_parts(x):
    first = x.astype(jnp.bfloat16).astype(jnp.float32)
    second = (x - first).astype(jnp.bfloat16).astype(jnp.float32)
    return first, second, x - first - second


def iota(shape, dim):
    return lax.broadcasted_iota(jnp.int32, shape, dim)


def device_at(place):
    return place % RINGS * RING + place // RINGS


def prepare_kernel(
    lengths_ref, source_ref, q0_ref, q1_ref, q_out, bias_out, doc_out
):
    me = lax.axis_index("ctx")
    lane = iota((ROWS, 128), 1)
    row = iota((ROWS, 128), 0)
    local = as_bf16(source_ref[...] - iota((CTX, 128), 1) // 2 * ROWS)
    spread = as_bf16(device_at(iota((ROWS, CTX), 0) // 2) == iota((ROWS, CTX), 1))
    table = jnp.dot(spread, local, preferred_element_type=jnp.float32)
    in_ring = me % RING
    base = me - in_ring
    for part, rows_ref in enumerate((q0_ref, q1_ref)):
        chunk = me + RING * part
        pick = jnp.sum(
            jnp.where(lane == 2 * chunk + row % 2, table, 0.0), axis=1, keepdims=True
        ).astype(jnp.int32)
        q_all = jnp.dot(as_bf16(lane == pick), rows_ref[...], preferred_element_type=jnp.float32)
        for h in range(HEADS):
            q_out[part, h * ROWS : (h + 1) * ROWS, :] = q_all[:, h * HD : (h + 1) * HD].astype(
                jnp.bfloat16
            )
        pos = chunk * ROWS + pick
        start = jnp.zeros_like(pos)
        doc = jnp.zeros_like(pos)
        end = jnp.int32(0)
        for i in range(DOCS):
            end = end + lengths_ref[i]
            passed = pos >= end
            start = jnp.where(passed, end, start)
            doc = doc + passed.astype(jnp.int32)
        doc_out[part] = jnp.broadcast_to(doc, (ROWS, 128))
        for j in range(RING + part):
            if j == RING:
                block = me
            else:
                block = base + j - jnp.where(j + part > in_ring, RING, 0)
            key_pos = block * ROWS + lane
            ok = (key_pos >= start) & (key_pos <= pos)
            bias_out[part, :, j * 128 : (j + 1) * 128] = jnp.where(ok, 0.0, NEG_BIG)


def attend_kernel(q_ref, bias_ref, doc_ref, kv_ref, own_ref, out_ref, kv_scr):
    lane = iota((ROWS, 128), 1)
    n = HEADS_AT_ONCE
    kv_scr[...] = kv_ref[...]
    kv_scr[pl.ds(pl.multiple_of(lax.axis_index("ctx") % RING * ROWS, ROWS), ROWS), :] = own_ref[...]
    all_peaks = [jnp.full((ROWS, 128), NEG_BIG, jnp.float32)] * PARTS
    all_logs = [jnp.full((ROWS, 128), NEG_BIG, jnp.float32)] * PARTS
    sources = [[(kv_scr, 0, FAR)], [(kv_ref, 0, FAR), (own_ref, FAR, WINDOW)]]

    def scores_of(part, h0):
        q = q_ref[part, h0 * ROWS : (h0 + n) * ROWS, :]
        return [
            dot_nt(q, ref[:, :HD]).reshape(n, ROWS, high - low) + bias_ref[part, :, low:high][None]
            for ref, low, high in sources[part]
        ]

    jobs = [(part, h0) for part in range(PARTS) for h0 in range(0, HEADS, n)]
    ahead = scores_of(*jobs[0])
    for i, (part, h0) in enumerate(jobs):
        scores = ahead
        if i + 1 < len(jobs):
            ahead = scores_of(*jobs[i + 1])
        tops = [jnp.max(s, axis=2, keepdims=True) for s in scores]
        top = tops[0] if part == 0 else jnp.maximum(tops[0], tops[1])
        weights = [jnp.exp2((s - top) * SCALE_LOG2E) for s in scores]
        total = sum(jnp.sum(w, axis=2, keepdims=True) for w in weights)
        acc = sum(
            jnp.dot(
                w.astype(jnp.bfloat16).reshape(n * ROWS, high - low),
                ref[:, HD:],
                preferred_element_type=jnp.float32,
            )
            for w, (ref, low, high) in zip(weights, sources[part])
        )
        context = acc.reshape(n, ROWS, HD) * (1.0 / total)
        for k in range(n):
            h = h0 + k
            at = part * WIDE + h * HD
            out_ref[:, at : at + HD] = context[k].astype(jnp.bfloat16)
            peak = top[k] * SCALE
            all_peaks[part] = jnp.where(lane % 8 == h, peak, all_peaks[part])
            all_logs[part] = jnp.where(lane % 8 == h, peak + jnp.log(total[k]), all_logs[part])
    best = jnp.full((ROWS, 128), NEG_BIG, jnp.float32)
    for part in range(PARTS):
        best = jnp.maximum(best, jnp.where(lane // 8 == doc_ref[part], all_peaks[part], NEG_BIG))

    logs = jnp.where(lane < 24, all_logs[0], all_logs[1])
    step = lane % 24 // 8
    pieces = three_parts(logs)
    tail = jnp.where(step == 0, pieces[0], jnp.where(step == 1, pieces[1], pieces[2]))
    most = three_parts(pltpu.roll(jnp.max(best, axis=0, keepdims=True), 48, 1))
    maxima = jnp.where(iota((ROWS, 128), 0) % 2 == 0, most[0], most[1])
    tail = jnp.where(lane < 48, tail, jnp.where(lane < 112, maxima, 0.0))
    out_ref[:, PARTS * WIDE :] = tail.astype(jnp.bfloat16)


def maxima_kernel(tail_ref, maxima_ref):
    row = iota((ROWS, 128), 0)
    tail = tail_ref[:, PARTS * WIDE :].astype(jnp.float32)

    most = tail + pltpu.roll(tail, ROWS - 1, 0)
    most = jnp.max(jnp.where(row % 2 == 0, most, NEG_BIG), axis=0, keepdims=True)
    lane_d = iota((DOCS, 128), 1)
    spread = jnp.where(lane_d // HEADS - 6 == iota((DOCS, 128), 0), most, 0.0)
    fold = as_bf16(iota((128, SPAN), 0) % HEADS == iota((128, SPAN), 1) % HEADS)
    folded = [
        jnp.dot(piece.astype(jnp.bfloat16), fold, preferred_element_type=jnp.float32)
        for piece in three_parts(spread)
    ]
    mine = iota((DOCS, SPAN), 1) // HEADS == lax.axis_index("head")
    maxima_ref[...] = jnp.where(mine, folded[0] + (folded[1] + folded[2]), 0.0)


def merge_kernel(got_ref, out_ref):
    row = iota((ROWS, 128), 0)

    to = iota((ROWS, ROWS), 0)
    source = to // 2 % RING * 2 * RINGS + to // (2 * RING) * 2 + to % 2
    from_near = as_bf16(iota((ROWS, ROWS), 1) == source)
    from_far = as_bf16(iota((ROWS, ROWS), 1) == source - 2)

    def ordered(rows, low, high):
        return jnp.dot(rows, got_ref[:, low:high], preferred_element_type=jnp.float32)

    tails = [ordered(rows, PARTS * WIDE, PARTS * WIDE + 128) for rows in (from_near, from_far)]

    def summed(tail):
        return tail + (pltpu.roll(tail, 128 - 8, 1) + pltpu.roll(tail, 128 - 16, 1))

    log_far = pltpu.roll(summed(tails[1]), 128 - 24, 1)
    share = 1.0 / (1.0 + jnp.exp(log_far - summed(tails[0])))
    share = jnp.where(row < 2 * RING, 1.0, share)
    for h in range(0, HEADS, 2):
        low, high = h * HD, (h + 2) * HD
        near = ordered(from_near, low, high)
        far = ordered(from_far, WIDE + low, WIDE + high)
        for k in range(2):
            w = share[:, h + k : h + k + 1]
            at = slice(k * HD, (k + 1) * HD)
            out_ref[:, low + k * HD : low + (k + 1) * HD] = (
                near[:, at] * w + far[:, at] * (1.0 - w)
            ).astype(jnp.bfloat16)


VMEM = pl.BlockSpec(memory_space=pltpu.VMEM)
SMEM = pl.BlockSpec(memory_space=pltpu.SMEM)
PARAMS = pltpu.CompilerParams(vmem_limit_bytes=40 * 1024 * 1024)
MERGE_COST = pl.CostEstimate(flops=10**8, bytes_accessed=10**7, transcendentals=0)


def body(queries, keys, values, doc_lengths, source_row):
    along_ring = [[r * RING + z for z in range(RING)] for r in range(RINGS)]

    def exchange(x, groups):
        return lax.all_to_all(
            x, "ctx", split_axis=0, concat_axis=0, tiled=True, axis_index_groups=groups
        )

    own = jnp.pad(keys, ((0, 0), (0, HD))) + jnp.pad(values, ((0, 0), (HD, 0)))
    before = lax.ppermute(own, "ctx", [(c, c + RING) for c in range(CTX - RING)])
    next_queries = lax.ppermute(queries, "ctx", [(c + RING, c) for c in range(CTX - RING)])
    later = jnp.arange(RING, dtype=jnp.int32) > lax.axis_index("ctx") % RING
    slots = jnp.where(later[:, None, None], own[None], before[None])
    window = exchange(slots, along_ring).reshape(FAR, 2 * HD)
    q_rows, bias, doc = pl.pallas_call(
        prepare_kernel,
        out_shape=(
            jax.ShapeDtypeStruct((PARTS, HEADS * ROWS, HD), jnp.bfloat16),
            jax.ShapeDtypeStruct((PARTS, ROWS, WINDOW), jnp.float32),
            jax.ShapeDtypeStruct((PARTS, ROWS, 128), jnp.int32),
        ),
        in_specs=[SMEM, VMEM, VMEM, VMEM],
        out_specs=(VMEM, VMEM, VMEM),
        compiler_params=PARAMS,
        name="prepare",
    )(doc_lengths, source_row, queries, next_queries)
    wide = PARTS * WIDE + 128
    sent = pl.pallas_call(
        attend_kernel,
        out_shape=jax.ShapeDtypeStruct((ROWS, wide), jnp.bfloat16),
        in_specs=[VMEM, VMEM, VMEM, VMEM, VMEM],
        out_specs=VMEM,
        scratch_shapes=[pltpu.VMEM((FAR, 2 * HD), jnp.bfloat16)],
        compiler_params=PARAMS,
        name="attend",
    )(q_rows, bias, doc, window, own)
    got = lax.all_to_all(
        sent.reshape(CTX, 2, wide),
        "ctx",
        split_axis=0,
        concat_axis=0,
        tiled=True,
        axis_index_groups=[[r * RING + z for z in range(RING) for r in ORDER]],
    )
    got = got.reshape(ROWS, wide)
    maxima = pl.pallas_call(
        maxima_kernel,
        out_shape=jax.ShapeDtypeStruct((DOCS, SPAN), jnp.float32),
        in_specs=[VMEM],
        out_specs=VMEM,
        compiler_params=PARAMS,
        name="maxima",
    )(got)
    everyone = maxima
    for k in range(1, GROUPS):
        everyone = everyone + lax.ppermute(
            maxima, "head", [(i, (i + k) % GROUPS) for i in range(GROUPS)]
        )
    context = pl.pallas_call(
        merge_kernel,
        out_shape=jax.ShapeDtypeStruct((ROWS, WIDE), jnp.bfloat16),
        in_specs=[VMEM],
        out_specs=VMEM,
        cost_estimate=MERGE_COST,
        compiler_params=PARAMS,
        name="merge",
    )(got)
    return (context, everyone.T)


def solution(mesh):
    return jax.shard_map(
        body,
        mesh=mesh,
        in_specs=(P("ctx", "head"), P("ctx", "head"), P("ctx", "head"), P(), P()),
        out_specs=(P("ctx", "head"), P()),
        check_vma=False,
    )
```
